1024 devices in a mesh: inner: 16 (over z_hi, x), outer: 64 (over z_lo, y, core).
Axes of the slice: x: 8, y: 8, z: 8 (z_hi: 2, z_lo: 4; z = z_hi * 4 + z_lo), core: 2. Of those that a mesh axis runs over, the one named last changes fastest.
Arguments:
- activations: bfloat16 [131072, 8192], P(('inner', 'outer')), may hold values from -6 to 6
- cotangent: bfloat16 [131072, 256], P(('inner', 'outer')), may hold values from -6 to 6
- token_ids: int32 [131072], P(('inner', 'outer')), may hold values from 0 to 128255, as said below
- kept_rows: int32 [2, 32], replicated, may hold values from 0 to 63, as said below
Outputs:
- grad_blocks: float32 [8192, 128], P(('inner', 'outer'))
The draws below stay inside these ranges and needn't reach their ends.
Inputs may be any that keep to these rules, and one draw needn't show every extreme that they name: `token_ids`: in each of the runs of 128 tokens that one device holds, the last 1 to 64 tokens are padding with id 0 and no other token has id 0. `kept_rows`: each row lists 32 distinct block rows in increasing order.
All inputs are finite; a program needn't handle non-finite values.
Results may differ from the reference program's by a relative error of at most 0.0003.
Values sent between devices are 32-bit elements; how exact they have to be, the bound alone decides.
No kernel may reach another device: no remote copies, remote signals or barrier semaphores. Data moves between devices by JAX's collectives and lax.ppermute only.
A program may use at most 32 MiB of HBM per device.

```python
import math
import jax
import jax.numpy as jnp
from jax import lax

D = 8192
VOCAB = 128256
BLOCK = 128
CB = 2
TOK_DEV = 128
KEPT = 32
TOKENS = 131072


def draw_token_ids(key, part):
    key = jax.random.fold_in(key, 11)
    length_key, id_key, spot_key, device_key = jax.random.split(key, 4)
    device_count = TOKENS // TOK_DEV
    pad_length = jax.random.randint(length_key, (device_count, 1), 1, TOK_DEV // 2 + 1)
    positions = jnp.arange(TOK_DEV, dtype=jnp.int32)[None, :]
    raw_ids = jax.random.randint(id_key, (device_count, TOK_DEV), 1, VOCAB)
    chosen_device = jax.random.randint(device_key, (), 0, device_count)
    chosen_spot = jax.random.randint(spot_key, (), 0, TOK_DEV // 2)
    devices = jnp.arange(device_count, dtype=jnp.int32)[:, None]
    marked = jnp.logical_and(devices == chosen_device, positions == chosen_spot)
    raw_ids = jnp.where(marked, VOCAB - 1, raw_ids)
    padded = jnp.where(positions >= TOK_DEV - pad_length, 0, raw_ids)
    return padded.reshape(TOKENS).astype(jnp.int32)


def pick_rows(key):
    block_rows = D // BLOCK
    shuffled = jax.random.permutation(key, block_rows - 2) + 1
    chosen = shuffled[:KEPT - 2]
    whole = jnp.concatenate([jnp.zeros((1,), jnp.int32), chosen.astype(jnp.int32), jnp.full((1,), block_rows - 1, jnp.int32)])
    return jnp.sort(whole)


def draw_kept_rows(key, part):
    key = jax.random.fold_in(key, 23)
    column_keys = jax.random.split(key, CB)
    return jax.vmap(pick_rows)(column_keys).astype(jnp.int32)


def block_scale(key, extent, shards, low, largest):
    level, own = 1.0, jax.random.fold_in(key, 6)
    for axis_at, shards_of in shards:
        draws = jnp.exp(jax.random.uniform(jax.random.fold_in(own, axis_at), (shards_of,), jnp.float32, low / len(shards), largest / len(shards)))
        level = level * jnp.repeat(draws, extent[axis_at] // shards_of).reshape([-1 if axis == axis_at else 1 for axis in range(len(extent))])
    return level


def scatter_about(rng, shape, spread, limit, pieces=(), kind=jnp.bfloat16):
    drawn = jax.random.normal(rng, shape, jnp.float32) * spread
    if len(pieces) > 0:
        drawn = block_scale(rng, shape, pieces, -0.22, 0.18) * drawn
    return jnp.clip(drawn, min=-limit, max=limit).astype(kind)


def setup_inputs(seed: int = 0) -> dict:
    key_list = jax.random.split(jax.random.key(seed), 5)
    return {
        "activations": scatter_about(key_list[0], (TOKENS, D), 1.0, 6.0, ((0, 1024),)),
        "cotangent": scatter_about(key_list[1], (TOKENS, CB * BLOCK), 1.0, 6.0, ((0, 1024),)),
        "token_ids": draw_token_ids(jax.random.fold_in(key_list[4], 71), 0),
        "kept_rows": draw_kept_rows(jax.random.fold_in(key_list[4], 71), 0),
    }


def reference(activations, cotangent, token_ids, kept_rows):
    live_grad = jnp.where((token_ids != 0)[:, None], cotangent, jnp.zeros_like(cotangent))
    step_rows = math.gcd(TOKENS, 4096)
    step_count = TOKENS // step_rows
    flat_kept = kept_rows.reshape(-1).astype(jnp.int32)

    def accumulate(carry, index):
        start_row = (index * step_rows).astype(jnp.int32)
        rows_x = lax.dynamic_slice_in_dim(activations, start_row, step_rows, 0)
        rows_g = lax.dynamic_slice_in_dim(live_grad, start_row, step_rows, 0)
        picked = jnp.take(rows_x.reshape(step_rows, D // BLOCK, BLOCK), flat_kept, axis=1)
        picked = picked.reshape(step_rows, CB, KEPT, BLOCK).astype(jnp.float32)
        targets = rows_g.reshape(step_rows, CB, BLOCK).astype(jnp.float32)
        return (carry + jnp.einsum('tjki,tjc->jkic', picked, targets), None)
    initial = jnp.zeros((CB, KEPT, BLOCK, BLOCK), jnp.float32)
    total, unused = lax.scan(accumulate, initial, jnp.arange(step_count, dtype=jnp.int32))
    return total.reshape(CB * KEPT * BLOCK, BLOCK) / jnp.sqrt(jnp.float32(TOKENS))
```

```python
import math

import jax
import jax.numpy as jnp
import numpy as np
from jax import lax
from jax.experimental import pallas as pl
from jax.experimental.pallas import tpu as pltpu
from jax.sharding import Mesh, PartitionSpec as P

ZH, X, ZL, Y, C = 2, 8, 4, 8, 2
Z = ZH * ZL
ALL = ZH * X * ZL * Y * C
ROWS = 8


def number(x, y, z, c):
    return (((z // ZL * X + x) * ZL + z % ZL) * Y + y) * C + c


def line(axis, x, y, z, c):
    if axis == "x":
        return [number(i, y, z, c) for i in range(X)]
    if axis == "y":
        return [number(x, i, z, c) for i in range(Y)]
    return [number(x, y, i, c) for i in range(Z)]


def lines(axis_of_core):
    groups = {
        tuple(line(axis_of_core[c], x, y, z, c))
        for x in range(X)
        for y in range(Y)
        for z in range(Z)
        for c in range(C)
    }
    return [list(g) for g in sorted(groups)]


def products(kept_ref, ids_ref, grad_ref, act_ref, mine_ref, send_ref):
    core = lax.rem(lax.axis_index("d"), C)
    width = ids_ref.shape[1]
    live = jnp.transpose(jnp.broadcast_to(ids_ref[...], (width, width))) != 0
    targets = [
        jnp.where(live, grad_ref[:, j * width:(j + 1) * width].astype(jnp.float32), 0.0).astype(jnp.bfloat16)
        for j in range(ZH)
    ]

    def run(own):
        zero_ref, one_ref = (mine_ref, send_ref) if own == 0 else (send_ref, mine_ref)

        def step(k, carry):
            x, zl = k // ZL, lax.rem(k, ZL)
            for j in range(ZH):
                z = j * ZL + zl
                start = pl.multiple_of(kept_ref[j, k] * width, width)
                block = act_ref[:, pl.ds(start, width)]
                sums = lax.dot_general(
                    block, targets[j], (((0,), (0,)), ((), ())), preferred_element_type=jnp.float32
                ).reshape(Y, C, ROWS, width)
                zero_ref[x, :, z] = sums[:, 0]
                one_ref[:, z, x] = sums[:, 1]
            return carry

        lax.fori_loop(0, X * ZL, step, 0, unroll=4)

    pl.when(core == 0)(lambda: run(0))
    pl.when(core == 1)(lambda: run(1))


def local(activations, cotangent, token_ids, kept_rows):
    tokens = activations.shape[0]
    tile = (ROWS, tokens)
    vmem = pl.BlockSpec(memory_space=pltpu.VMEM)
    mine, send = pl.pallas_call(
        products,
        out_shape=[jax.ShapeDtypeStruct((8, 8, 8) + tile, jnp.float32)] * 2,
        in_specs=[pl.BlockSpec(memory_space=pltpu.SMEM), vmem, vmem, vmem],
        out_specs=[vmem, vmem],
        compiler_params=pltpu.CompilerParams(vmem_limit_bytes=48 * 1024 * 1024),
        name="products",
    )(kept_rows, token_ids.reshape(1, tokens), cotangent, activations)
    other = lax.ppermute(send, "d", [(i, i ^ 1) for i in range(ALL)])
    held = mine + other
    for axes in (("x", "y"), ("y", "z"), ("z", "x")):
        parts = lax.all_to_all(
            held, "d", split_axis=0, concat_axis=0, axis_index_groups=lines(axes), tiled=True
        )
        held = jnp.sum(parts, axis=0)
    return held * jnp.float32(1.0 / math.sqrt(tokens * ALL))


def solution(mesh):
    flat = Mesh(np.asarray(mesh.devices).reshape(-1), ("d",))
    in_specs = (P("d", None), P("d", None), P("d"), P())
    return jax.shard_map(local, mesh=flat, in_specs=in_specs, out_specs=P("d", None), check_vma=False)
```

```python
import math

import jax
import jax.numpy as jnp
import numpy as np
from jax import lax
from jax.experimental import pallas as pl
from jax.experimental.pallas import tpu as pltpu
from jax.sharding import Mesh, PartitionSpec as P

ZH, X, ZL, Y, C = 2, 8, 4, 8, 2
Z = ZH * ZL
ALL = ZH * X * ZL * Y * C
ROWS = 8


def number(x, y, z, c):
    return (((z // ZL * X + x) * ZL + z % ZL) * Y + y) * C + c


def cubes():
    groups = []
    for c in range(C):
        for x in range(c, X, 2):
            for y in range(c, Y, 2):
                for z in range(c, Z, 2):
                    members = [((x + i) % X, (y + j) % Y, (z + k) % Z) for i in range(2) for j in range(2) for k in range(2)]
                    members.sort(key=lambda m: (m[0] % 2, m[1] % 2, m[2] % 2))
                    groups.append([number(*m, c) for m in members])
    return groups


def lattices():
    return [
        [number(x, y, z, c) for x in range(i, X, 2) for y in range(j, Y, 2) for z in range(k, Z, 2)]
        for c in range(C)
        for i in range(2)
        for j in range(2)
        for k in range(2)
    ]


def products(kept_ref, ids_ref, grad_ref, act_ref, mine_ref, send_ref):
    core = lax.rem(lax.axis_index("d"), C)
    width = ids_ref.shape[1]
    live = jnp.transpose(jnp.broadcast_to(ids_ref[...], (width, width))) != 0
    targets = [
        jnp.where(live, grad_ref[:, j * width:(j + 1) * width].astype(jnp.float32), 0.0).astype(jnp.bfloat16)
        for j in range(ZH)
    ]

    def run(own):
        zero_ref, one_ref = (mine_ref, send_ref) if own == 0 else (send_ref, mine_ref)

        def step(k, carry):
            x, zl = k // ZL, lax.rem(k, ZL)
            for j in range(ZH):
                z = j * ZL + zl
                start = pl.multiple_of(kept_ref[j, k] * width, width)
                block = act_ref[:, pl.ds(start, width)]
                sums = lax.dot_general(
                    block, targets[j], (((0,), (0,)), ((), ())), preferred_element_type=jnp.float32
                ).reshape(Y // 2, 2, C, ROWS, width)
                for odd in range(2):
                    zero_ref[x % 2, odd, z % 2, x // 2, :, z // 2] = sums[:, odd, 0]
                    one_ref[x % 2, odd, z % 2, x // 2, :, z // 2] = sums[:, odd, 1]
            return carry

        lax.fori_loop(0, X * ZL, step, 0, unroll=4)

    pl.when(core == 0)(lambda: run(0))
    pl.when(core == 1)(lambda: run(1))


def local(activations, cotangent, token_ids, kept_rows):
    tokens = activations.shape[0]
    tile = (ROWS, tokens)
    vmem = pl.BlockSpec(memory_space=pltpu.VMEM)
    mine, send = pl.pallas_call(
        products,
        out_shape=[jax.ShapeDtypeStruct((2, 2, 2, X // 2, Y // 2, Z // 2) + tile, jnp.float32)] * 2,
        in_specs=[pl.BlockSpec(memory_space=pltpu.SMEM), vmem, vmem, vmem],
        out_specs=[vmem, vmem],
        compiler_params=pltpu.CompilerParams(vmem_limit_bytes=48 * 1024 * 1024),
        name="products",
    )(kept_rows, token_ids.reshape(1, tokens), cotangent, activations)
    other = lax.ppermute(send, "d", [(i, i ^ 1) for i in range(ALL)])
    held = (mine + other).reshape((-1,) + tile)
    for groups in (cubes(), lattices()):
        parts = lax.all_to_all(held, "d", split_axis=0, concat_axis=0, axis_index_groups=groups, tiled=True)
        held = jnp.sum(parts.reshape((len(groups[0]), -1) + tile), axis=0)
    held = held.reshape(tile)
    return held * jnp.float32(1.0 / math.sqrt(tokens * ALL))


def solution(mesh):
    flat = Mesh(np.asarray(mesh.devices).reshape(-1), ("d",))
    in_specs = (P("d", None), P("d", None), P("d"), P())
    return jax.shard_map(local, mesh=flat, in_specs=in_specs, out_specs=P("d", None), check_vma=False)
```

```python
import math

import jax
import jax.numpy as jnp
import numpy as np
from jax import lax
from jax.experimental import pallas as pl
from jax.experimental.pallas import tpu as pltpu
from jax.sharding import Mesh, PartitionSpec as P

ZH, X, ZL, Y, C = 2, 8, 4, 8, 2
Z = ZH * ZL
ALL = ZH * X * ZL * Y * C
ROWS = 8


def number(x, y, z, c):
    return (((z // ZL * X + x) * ZL + z % ZL) * Y + y) * C + c


def bit(value, at):
    return value >> at & 1


def exchanges():
    keys = []
    for c in range(C):
        first = lambda x, y, z, c=c: (c, (x - c) % X // 2, (y - c) % Y // 2, (z - c) % Z // 2)
        keys.append(first)
    found = [{}, {}, {}]
    for c in range(C):
        for x in range(X):
            for y in range(Y):
                for z in range(Z):
                    a, b, d = (x, y, z) if c == 0 else (y, z, x)
                    odd = (x % 2, y % 2, z % 2)
                    second, third = (a // 2, bit(b, 1)), (d // 2, bit(b, 2))
                    for groups, group, place in zip(
                        found,
                        (keys[c](x, y, z), (c, odd, third), (c, odd, second)),
                        (odd, second, third),
                        strict=True,
                    ):
                        groups.setdefault(group, []).append((place, number(x, y, z, c)))
    return [[[n for _, n in sorted(g)] for g in groups.values()] for groups in found]


def products(kept_any, ids_any, grad_any, act_any, mine_ref, send_ref, kept_ref, ids_ref, grad_ref, act_ref, sems):
    copies = [
        pltpu.make_async_copy(src, dst, sems.at[i])
        for i, (src, dst) in enumerate(
            ((act_any, act_ref), (kept_any, kept_ref), (ids_any, ids_ref), (grad_any, grad_ref))
        )
    ]
    for copy in copies:
        copy.start()
    core = lax.rem(lax.axis_index("d"), C)
    tokens, width = act_ref.shape[0], grad_ref.shape[1] // ZH
    scale = 1.0 / math.sqrt(tokens * ALL)
    for copy in copies[1:]:
        copy.wait()
    live = jnp.transpose(jnp.broadcast_to(ids_ref[...], (width, tokens))) != 0
    targets = [
        jnp.where(live, grad_ref[:, j * width:(j + 1) * width].astype(jnp.float32), 0.0).astype(jnp.bfloat16)
        for j in range(ZH)
    ]
    copies[0].wait()

    def run(own):
        zero_ref, one_ref = (mine_ref, send_ref) if own == 0 else (send_ref, mine_ref)

        def step(k, carry):
            x, zl = k // ZL, lax.rem(k, ZL)
            xo, xh, zo, z1 = x % 2, x // 2, zl % 2, zl // 2
            for j in range(ZH):
                start = pl.multiple_of(kept_ref[j, k] * width, width)
                block = act_ref[:, pl.ds(start, width)]
                sums = lax.dot_general(
                    block, targets[j], (((0,), (0,)), ((), ())), preferred_element_type=jnp.float32
                ) * jnp.float32(scale)
                sums = sums.reshape(Y // 2, 2, C, ROWS, width)
                for yo in range(2):
                    one_ref[xo, yo, zo, :, z1, xh, j] = sums[:, yo, 1]
                    halves = sums[:, yo, 0].reshape(2, 2, ROWS, width)
                    for y1 in range(2):
                        zero_ref[xo, yo, zo, xh, y1, j * 2 + z1] = halves[:, y1]
            return carry

        lax.fori_loop(0, X * ZL, step, 0, unroll=4)

    pl.when(core == 0)(lambda: run(0))
    pl.when(core == 1)(lambda: run(1))


def local(activations, cotangent, token_ids, kept_rows):
    tokens = activations.shape[0]
    tile = (ROWS, cotangent.shape[1] // ZH)
    vmem, hbm = pl.BlockSpec(memory_space=pltpu.VMEM), pl.BlockSpec(memory_space=pltpu.HBM)
    mine, send = pl.pallas_call(
        products,
        out_shape=[jax.ShapeDtypeStruct((2, 2, 2, 4, 2, 4, 2) + tile, jnp.float32)] * 2,
        in_specs=[hbm] * 4,
        out_specs=[vmem, vmem],
        scratch_shapes=[
            pltpu.SMEM(kept_rows.shape, jnp.int32),
            pltpu.VMEM((1, tokens), jnp.int32),
            pltpu.VMEM(cotangent.shape, jnp.bfloat16),
            pltpu.VMEM(activations.shape, jnp.bfloat16),
            pltpu.SemaphoreType.DMA((4,)),
        ],
        compiler_params=pltpu.CompilerParams(vmem_limit_bytes=48 * 1024 * 1024),
        name="products",
    )(*(
        pltpu.with_memory_space_constraint(a, pltpu.HBM)
        for a in (kept_rows, token_ids.reshape(1, tokens), cotangent, activations)
    ))
    other = lax.ppermute(send, "d", [(i, i ^ 1) for i in range(ALL)])
    held = (mine + other).reshape((-1,) + tile)
    for groups in exchanges():
        parts = lax.all_to_all(held, "d", split_axis=0, concat_axis=0, axis_index_groups=groups, tiled=True)
        held = jnp.sum(parts.reshape((len(groups[0]), -1) + tile), axis=0)
    return held.reshape(tile)


def solution(mesh):
    flat = Mesh(np.asarray(mesh.devices).reshape(-1), ("d",))
    in_specs = (P("d", None), P("d", None), P("d"), P())
    return jax.shard_map(local, mesh=flat, in_specs=in_specs, out_specs=P("d", None), check_vma=False)
```

```python
import math

import jax
import jax.numpy as jnp
import numpy as np
from jax import lax
from jax.experimental import pallas as pl
from jax.experimental.pallas import tpu as pltpu
from jax.sharding import Mesh, PartitionSpec as P

ZH, X, ZL, Y, C = 2, 8, 4, 8, 2
Z = ZH * ZL
ALL = ZH * X * ZL * Y * C
ROWS = 8


def number(x, y, z, c):
    return (((z // ZL * X + x) * ZL + z % ZL) * Y + y) * C + c


def half(place):
    return (place ^ place >> 1 ^ place >> 2) & 1


def order(x, y, z):
    return half(x) * 4 + half(y) * 2 + half(z), x // 2 * 16 + y // 2 * 4 + z // 2


def exchanges():
    cubes, lattices = {}, {}
    for c in range(C):
        for x in range(X):
            for y in range(Y):
                for z in range(Z):
                    first, second = order(x, y, z)
                    device = number((x + c) % X, (y + c) % Y, (z + c) % Z, c)
                    cubes.setdefault((c, second), []).append((first, device))
                    lattices.setdefault((c, first), []).append((second, device))
    return [[[n for _, n in sorted(g)] for g in groups.values()] for groups in (cubes, lattices)]


def products(kept_any, ids_any, grad_any, act_any, mine_ref, send_ref, kept_ref, ids_ref, grad_ref, act_ref, sems):
    copies = [
        pltpu.make_async_copy(src, dst, sems.at[i])
        for i, (src, dst) in enumerate(
            ((act_any, act_ref), (kept_any, kept_ref), (ids_any, ids_ref), (grad_any, grad_ref))
        )
    ]
    for copy in copies:
        copy.start()
    core = lax.rem(lax.axis_index("d"), C)
    tokens, width = act_ref.shape[0], grad_ref.shape[1] // ZH
    scale = 1.0 / math.sqrt(tokens * ALL)
    for copy in copies[1:]:
        copy.wait()
    live = jnp.transpose(jnp.broadcast_to(ids_ref[...], (width, tokens))) != 0
    targets = [
        jnp.where(live, grad_ref[:, j * width:(j + 1) * width].astype(jnp.float32), 0.0).astype(jnp.bfloat16)
        for j in range(ZH)
    ]
    copies[0].wait()

    def run(own):
        zero_ref, one_ref = (mine_ref, send_ref) if own == 0 else (send_ref, mine_ref)

        def step(x, carry):
            for z in range(Z):
                j, k = z // ZL, x * ZL + z % ZL
                start = pl.multiple_of(kept_ref[j, k] * width, width)
                block = act_ref[:, pl.ds(start, width)]
                sums = lax.dot_general(
                    block, targets[j], (((0,), (0,)), ((), ())), preferred_element_type=jnp.float32
                ) * jnp.float32(scale)
                sums = sums.reshape(Y, C, ROWS, width)
                for c, ref in enumerate((zero_ref, one_ref)):
                    xc, zc = (x + X - c) % X, (z - c) % Z
                    for y in range(Y):
                        ref[order(xc, (y - c) % Y, zc)] = sums[y, c]
            return carry

        lax.fori_loop(0, X, step, 0)

    pl.when(core == 0)(lambda: run(0))
    pl.when(core == 1)(lambda: run(1))


def local(activations, cotangent, token_ids, kept_rows):
    tokens = activations.shape[0]
    tile = (ROWS, cotangent.shape[1] // ZH)
    vmem, hbm = pl.BlockSpec(memory_space=pltpu.VMEM), pl.BlockSpec(memory_space=pltpu.HBM)
    mine, send = pl.pallas_call(
        products,
        out_shape=[jax.ShapeDtypeStruct((8, ALL // C // 8) + tile, jnp.float32)] * 2,
        in_specs=[hbm] * 4,
        out_specs=[vmem, vmem],
        scratch_shapes=[
            pltpu.SMEM(kept_rows.shape, jnp.int32),
            pltpu.VMEM((1, tokens), jnp.int32),
            pltpu.VMEM(cotangent.shape, jnp.bfloat16),
            pltpu.VMEM(activations.shape, jnp.bfloat16),
            pltpu.SemaphoreType.DMA((4,)),
        ],
        compiler_params=pltpu.CompilerParams(vmem_limit_bytes=48 * 1024 * 1024),
        name="products",
    )(*(
        pltpu.with_memory_space_constraint(a, pltpu.HBM)
        for a in (kept_rows, token_ids.reshape(1, tokens), cotangent, activations)
    ))
    other = lax.ppermute(send, "d", [(i, i ^ 1) for i in range(ALL)])
    held = (mine + other).reshape((-1,) + tile)
    for groups in exchanges():
        parts = lax.all_to_all(held, "d", split_axis=0, concat_axis=0, axis_index_groups=groups, tiled=True)
        held = jnp.sum(parts.reshape((len(groups[0]), -1) + tile), axis=0)
    return held.reshape(tile)


def solution(mesh):
    flat = Mesh(np.asarray(mesh.devices).reshape(-1), ("d",))
    in_specs = (P("d", None), P("d", None), P("d"), P())
    return jax.shard_map(local, mesh=flat, in_specs=in_specs, out_specs=P("d", None), check_vma=False)
```

```python
import math

import jax
import jax.numpy as jnp
import numpy as np
from jax import lax
from jax.experimental import pallas as pl
from jax.experimental.pallas import tpu as pltpu
from jax.sharding import Mesh, PartitionSpec as P

ZH, X, ZL, Y, C = 2, 8, 4, 8, 2
Z = ZH * ZL
ALL = ZH * X * ZL * Y * C
ROWS = 8


def number(x, y, z, c):
    return (((z // ZL * X + x) * ZL + z % ZL) * Y + y) * C + c


def half(place):
    return (place ^ place >> 1 ^ place >> 2) & 1


def order(x, y, z):
    return half(x) * 4 + half(y) * 2 + half(z), x // 2 * 16 + y // 2 * 4 + z // 2


def exchanges():
    cubes, lattices = {}, {}
    for c in range(C):
        for x in range(X):
            for y in range(Y):
                for z in range(Z):
                    first, second = order(x, y, z)
                    device = number((x + c) % X, (y + c) % Y, (z + c) % Z, c)
                    cubes.setdefault((c, second), []).append((first, device))
                    lattices.setdefault((c, first), []).append((second, device))
    return [[[n for _, n in sorted(g)] for g in groups.values()] for groups in (cubes, lattices)]


def products(kept_any, ids_any, grad_any, act_any, mine_ref, send_ref, kept_ref, ids_ref, grad_ref, act_ref, sems):
    copies = [
        pltpu.make_async_copy(src, dst, sems.at[i])
        for i, (src, dst) in enumerate(
            ((act_any, act_ref), (kept_any, kept_ref), (ids_any, ids_ref), (grad_any, grad_ref))
        )
    ]
    for copy in copies:
        copy.start()
    core = lax.rem(lax.axis_index("d"), C)
    tokens, width = act_ref.shape[0], grad_ref.shape[1] // ZH
    scale = 1.0 / math.sqrt(tokens * ALL)
    for copy in copies[1:]:
        copy.wait()
    live = jnp.transpose(jnp.broadcast_to(ids_ref[...], (width, tokens))) != 0
    targets = [
        jnp.where(live, grad_ref[:, j * width:(j + 1) * width].astype(jnp.float32), 0.0).astype(jnp.bfloat16)
        for j in range(ZH)
    ]
    copies[0].wait()

    def run(own):
        zero_ref, one_ref = (mine_ref, send_ref) if own == 0 else (send_ref, mine_ref)

        def step(x, carry):
            for z in range(Z):
                j, k = z // ZL, x * ZL + z % ZL
                start = pl.multiple_of(kept_ref[j, k] * width, width)
                block = act_ref[:, pl.ds(start, width)]
                sums = lax.dot_general(
                    block, targets[j], (((0,), (0,)), ((), ())), preferred_element_type=jnp.float32
                ) * jnp.float32(scale)
                sums = sums.reshape(Y, C, ROWS, width)
                for c, ref in enumerate((zero_ref, one_ref)):
                    xc, zc = (x + X - c) % X, (z - c) % Z
                    for y in range(Y):
                        ref[order(xc, (y - c) % Y, zc)] = sums[y, c]
            return carry

        lax.fori_loop(0, X, step, 0, unroll=True)

    pl.when(core == 0)(lambda: run(0))
    pl.when(core == 1)(lambda: run(1))


def local(activations, cotangent, token_ids, kept_rows):
    tokens = activations.shape[0]
    tile = (ROWS, cotangent.shape[1] // ZH)
    vmem, hbm = pl.BlockSpec(memory_space=pltpu.VMEM), pl.BlockSpec(memory_space=pltpu.HBM)
    mine, send = pl.pallas_call(
        products,
        out_shape=[jax.ShapeDtypeStruct((8, ALL // C // 8) + tile, jnp.float32)] * 2,
        in_specs=[hbm] * 4,
        out_specs=[vmem, vmem],
        scratch_shapes=[
            pltpu.SMEM(kept_rows.shape, jnp.int32),
            pltpu.VMEM((1, tokens), jnp.int32),
            pltpu.VMEM(cotangent.shape, jnp.bfloat16),
            pltpu.VMEM(activations.shape, jnp.bfloat16),
            pltpu.SemaphoreType.DMA((4,)),
        ],
        compiler_params=pltpu.CompilerParams(vmem_limit_bytes=48 * 1024 * 1024),
        name="products",
    )(*(
        pltpu.with_memory_space_constraint(a, pltpu.HBM)
        for a in (kept_rows, token_ids.reshape(1, tokens), cotangent, activations)
    ))
    other = lax.ppermute(send, "d", [(i, i ^ 1) for i in range(ALL)])
    held = (mine + other).reshape((-1,) + tile)
    for groups in exchanges():
        parts = lax.all_to_all(held, "d", split_axis=0, concat_axis=0, axis_index_groups=groups, tiled=True)
        held = jnp.sum(parts.reshape((len(groups[0]), -1) + tile), axis=0)
    return held.reshape(tile)


def solution(mesh):
    flat = Mesh(np.asarray(mesh.devices).reshape(-1), ("d",))
    in_specs = (P("d", None), P("d", None), P("d"), P())
    return jax.shard_map(local, mesh=flat, in_specs=in_specs, out_specs=P("d", None), check_vma=False)
```

```python
import math

import jax
import jax.numpy as jnp
import numpy as np
from jax import lax
from jax.experimental import pallas as pl
from jax.experimental.pallas import tpu as pltpu
from jax.sharding import Mesh, PartitionSpec as P

ZH, X, ZL, Y, C = 2, 8, 4, 8, 2
Z = ZH * ZL
ALL = ZH * X * ZL * Y * C
ROWS = 8
START = ((0, 1, 1), (1, 0, 0))


def number(x, y, z, c):
    return (((z // ZL * X + x) * ZL + z % ZL) * Y + y) * C + c


def half(place):
    return (place ^ place >> 1 ^ place >> 2) & 1


def order(x, y, z):
    return half(x) * 4 + half(y) * 2 + half(z), x // 2 * 16 + y // 2 * 4 + z // 2


def exchanges():
    cubes, lattices = {}, {}
    for c in range(C):
        for x in range(X):
            for y in range(Y):
                for z in range(Z):
                    first, second = order(x, y, z)
                    device = number((x + START[c][0]) % X, (y + START[c][1]) % Y, (z + START[c][2]) % Z, c)
                    cubes.setdefault((c, second), []).append((first, device))
                    lattices.setdefault((c, first), []).append((second, device))
    return [[[n for _, n in sorted(g)] for g in groups.values()] for groups in (cubes, lattices)]


def products(kept_any, ids_any, grad_any, act_any, mine_ref, send_ref, kept_ref, ids_ref, grad_ref, act_ref, sems):
    copies = [
        pltpu.make_async_copy(src, dst, sems.at[i])
        for i, (src, dst) in enumerate(
            ((act_any, act_ref), (kept_any, kept_ref), (ids_any, ids_ref), (grad_any, grad_ref))
        )
    ]
    for copy in copies:
        copy.start()
    core = lax.rem(lax.axis_index("d"), C)
    tokens, width = act_ref.shape[0], grad_ref.shape[1] // ZH
    scale = 1.0 / math.sqrt(tokens * ALL)
    for copy in copies[1:]:
        copy.wait()
    live = jnp.transpose(jnp.broadcast_to(ids_ref[...], (width, tokens))) != 0
    targets = [
        jnp.where(live, grad_ref[:, j * width:(j + 1) * width].astype(jnp.float32), 0.0).astype(jnp.bfloat16)
        for j in range(ZH)
    ]
    copies[0].wait()

    def run(own):
        zero_ref, one_ref = (mine_ref, send_ref) if own == 0 else (send_ref, mine_ref)

        def step(x, carry):
            for z in range(Z):
                j, k = z // ZL, x * ZL + z % ZL
                start = pl.multiple_of(kept_ref[j, k] * width, width)
                block = act_ref[:, pl.ds(start, width)]
                sums = lax.dot_general(
                    block, targets[j], (((0,), (0,)), ((), ())), preferred_element_type=jnp.float32
                ) * jnp.float32(scale)
                sums = sums.reshape(Y, C, ROWS, width)
                for c, ref in enumerate((zero_ref, one_ref)):
                    xc, zc = (x + X - START[c][0]) % X, (z - START[c][2]) % Z
                    for y in range(Y):
                        ref[order(xc, (y - START[c][1]) % Y, zc)] = sums[y, c]
            return carry

        lax.fori_loop(0, X, step, 0, unroll=True)

    pl.when(core == 0)(lambda: run(0))
    pl.when(core == 1)(lambda: run(1))


def local(activations, cotangent, token_ids, kept_rows):
    tokens = activations.shape[0]
    tile = (ROWS, cotangent.shape[1] // ZH)
    vmem, hbm = pl.BlockSpec(memory_space=pltpu.VMEM), pl.BlockSpec(memory_space=pltpu.HBM)
    mine, send = pl.pallas_call(
        products,
        out_shape=[jax.ShapeDtypeStruct((8, ALL // C // 8) + tile, jnp.float32)] * 2,
        in_specs=[hbm] * 4,
        out_specs=[vmem, vmem],
        scratch_shapes=[
            pltpu.SMEM(kept_rows.shape, jnp.int32),
            pltpu.VMEM((1, tokens), jnp.int32),
            pltpu.VMEM(cotangent.shape, jnp.bfloat16),
            pltpu.VMEM(activations.shape, jnp.bfloat16),
            pltpu.SemaphoreType.DMA((4,)),
        ],
        compiler_params=pltpu.CompilerParams(vmem_limit_bytes=48 * 1024 * 1024),
        name="products",
    )(*(
        pltpu.with_memory_space_constraint(a, pltpu.HBM)
        for a in (kept_rows, token_ids.reshape(1, tokens), cotangent, activations)
    ))
    other = lax.ppermute(send, "d", [(i, i ^ 1) for i in range(ALL)])
    held = (mine + other).reshape((-1,) + tile)
    for groups in exchanges():
        parts = lax.all_to_all(held, "d", split_axis=0, concat_axis=0, axis_index_groups=groups, tiled=True)
        held = jnp.sum(parts.reshape((len(groups[0]), -1) + tile), axis=0)
    return held.reshape(tile)


def solution(mesh):
    flat = Mesh(np.asarray(mesh.devices).reshape(-1), ("d",))
    in_specs = (P("d", None), P("d", None), P("d"), P())
    return jax.shard_map(local, mesh=flat, in_specs=in_specs, out_specs=P("d", None), check_vma=False)
```

```python
import math

import jax
import jax.numpy as jnp
import numpy as np
from jax import lax
from jax.experimental import pallas as pl
from jax.experimental.pallas import tpu as pltpu
from jax.sharding import Mesh, PartitionSpec as P

ZH, X, ZL, Y, C = 2, 8, 4, 8, 2
Z = ZH * ZL
ALL = ZH * X * ZL * Y * C
ROWS = 8
START = ((0, 1, 1), (1, 0, 4))


def number(x, y, z, c):
    return (((z // ZL * X + x) * ZL + z % ZL) * Y + y) * C + c


def half(place):
    return (place ^ place >> 1 ^ place >> 2) & 1


def order(x, y, z):
    return half(x) * 4 + half(y) * 2 + half(z), x // 2 * 16 + y // 2 * 4 + z // 2


def exchanges():
    cubes, lattices = {}, {}
    for c in range(C):
        for x in range(X):
            for y in range(Y):
                for z in range(Z):
                    first, second = order(x, y, z)
                    device = number((x + START[c][0]) % X, (y + START[c][1]) % Y, (z + START[c][2]) % Z, c)
                    cubes.setdefault((c, second), []).append((first, device))
                    lattices.setdefault((c, first), []).append((second, device))
    return [[[n for _, n in sorted(g)] for g in groups.values()] for groups in (cubes, lattices)]


def products(kept_any, ids_any, grad_any, act_any, mine_ref, send_ref, kept_ref, ids_ref, grad_ref, act_ref, sems):
    copies = [
        pltpu.make_async_copy(src, dst, sems.at[i])
        for i, (src, dst) in enumerate(
            ((act_any, act_ref), (kept_any, kept_ref), (ids_any, ids_ref), (grad_any, grad_ref))
        )
    ]
    for copy in copies:
        copy.start()
    core = lax.rem(lax.axis_index("d"), C)
    tokens, width = act_ref.shape[0], grad_ref.shape[1] // ZH
    scale = 1.0 / math.sqrt(tokens * ALL)
    for copy in copies[1:]:
        copy.wait()
    live = jnp.transpose(jnp.broadcast_to(ids_ref[...], (width, tokens))) != 0
    targets = [
        jnp.where(live, grad_ref[:, j * width:(j + 1) * width].astype(jnp.float32), 0.0).astype(jnp.bfloat16)
        for j in range(ZH)
    ]
    copies[0].wait()

    def run(own):
        zero_ref, one_ref = (mine_ref, send_ref) if own == 0 else (send_ref, mine_ref)

        def step(x, carry):
            for z in range(Z):
                j, k = z // ZL, x * ZL + z % ZL
                start = pl.multiple_of(kept_ref[j, k] * width, width)
                block = act_ref[:, pl.ds(start, width)]
                sums = lax.dot_general(
                    block, targets[j], (((0,), (0,)), ((), ())), preferred_element_type=jnp.float32
                ) * jnp.float32(scale)
                sums = sums.reshape(Y, C, ROWS, width)
                for c, ref in enumerate((zero_ref, one_ref)):
                    xc, zc = (x + X - START[c][0]) % X, (z - START[c][2]) % Z
                    for y in range(Y):
                        ref[order(xc, (y - START[c][1]) % Y, zc)] = sums[y, c]
            return carry

        lax.fori_loop(0, X, step, 0, unroll=True)

    pl.when(core == 0)(lambda: run(0))
    pl.when(core == 1)(lambda: run(1))


def local(activations, cotangent, token_ids, kept_rows):
    tokens = activations.shape[0]
    tile = (ROWS, cotangent.shape[1] // ZH)
    vmem, hbm = pl.BlockSpec(memory_space=pltpu.VMEM), pl.BlockSpec(memory_space=pltpu.HBM)
    mine, send = pl.pallas_call(
        products,
        out_shape=[jax.ShapeDtypeStruct((8, ALL // C // 8) + tile, jnp.float32)] * 2,
        in_specs=[hbm] * 4,
        out_specs=[vmem, vmem],
        scratch_shapes=[
            pltpu.SMEM(kept_rows.shape, jnp.int32),
            pltpu.VMEM((1, tokens), jnp.int32),
            pltpu.VMEM(cotangent.shape, jnp.bfloat16),
            pltpu.VMEM(activations.shape, jnp.bfloat16),
            pltpu.SemaphoreType.DMA((4,)),
        ],
        compiler_params=pltpu.CompilerParams(vmem_limit_bytes=48 * 1024 * 1024),
        name="products",
    )(*(
        pltpu.with_memory_space_constraint(a, pltpu.HBM)
        for a in (kept_rows, token_ids.reshape(1, tokens), cotangent, activations)
    ))
    other = lax.ppermute(send, "d", [(i, i ^ 1) for i in range(ALL)])
    held = (mine + other).reshape((-1,) + tile)
    for groups in exchanges():
        parts = lax.all_to_all(held, "d", split_axis=0, concat_axis=0, axis_index_groups=groups, tiled=True)
        held = jnp.sum(parts.reshape((len(groups[0]), -1) + tile), axis=0)
    return held.reshape(tile)


def solution(mesh):
    flat = Mesh(np.asarray(mesh.devices).reshape(-1), ("d",))
    in_specs = (P("d", None), P("d", None), P("d"), P())
    return jax.shard_map(local, mesh=flat, in_specs=in_specs, out_specs=P("d", None), check_vma=False)
```
